256 devices in a mesh: dp: 8 (over x, core), bal: 32 (over y, z).
Axes of the slice: x: 4, y: 4, z: 8, core: 2. Of those that a mesh axis runs over, the one named last changes fastest.
Arguments:
- patches: bfloat16 [512, 256, 1152], P(('dp', 'bal')), parts along dimension 0, may hold values from -6 to 6
- counts: int32 [128], P('dp'), parts along dimension 0, may hold values from 1 to 8, 64 in all
- owner_pick: int32 [128], P('dp'), parts along dimension 0, may hold values from 0 to 59
- ln_gain: float32 [1152], replicated, may hold values from 0.1 to 1.9
- ln_bias: float32 [1152], replicated, may hold values from -3 to 3
- w_qkv: bfloat16 [1152, 1728], replicated, may hold values from -0.1875 to 0.1875
- w_out: bfloat16 [576, 1152], replicated, may hold values from -0.25 to 0.25
- ctx_gain: float32 [1152], replicated, may hold values from 0.1 to 1.9
- w_kv: bfloat16 [1152, 768], replicated, may hold values from -0.1875 to 0.1875
- latent_queries: bfloat16 [64, 1536], replicated, may hold values from -160 to 160
- latent_kv: bfloat16 [64, 768], replicated, may hold values from -6 to 6
Outputs:
- resampled: bfloat16 [256, 2, 64, 1536], P(('dp', 'bal')), parts along dimension 0
The draws below stay inside these ranges and needn't reach their ends.
There are 8 independent parts, one for each index of `dp`. The reference program is written for one: setup_inputs(seed, part) draws one part's arguments, and reference() takes and returns one part's arrays. A program takes and returns all parts, laid end to end along the dimension named above; an argument that names none is the same for every part. Nothing has to cross between parts.
Inputs may be any that keep to these rules, and one draw needn't show every extreme that they name: `owner_pick`: the choice of each image's owner among the devices holding its tiles.
All inputs are finite; a program needn't handle non-finite values.
Results may differ from the reference program's by a relative error of at most 0.02.
Values may be sent and summed in bfloat16 or wider, within the bound.
A program may use at most 128 MiB of HBM per device.

```python
import math
import jax
import jax.numpy as jnp
import numpy as np
from jax import lax

D = 1152
HA = 8
HS = 72
PATCHES = 256
QH = 16
KVH = 4
RD = 96
LAT = 64
TILE_DEV = 2
MAX_TILES = 8
TILES = 64
IMAGES = 16
N_BAL = 32


def shared_parts(key):
    base_key = jax.random.fold_in(key, 0)
    base = jnp.clip(jax.random.normal(base_key, (LAT, 2 * KVH * RD), jnp.float32), -6.0, 6.0)
    return base


def draw_latent_kv(key, part):
    base = shared_parts(key)
    return base.astype(jnp.bfloat16)


def draw_latent_queries(key, part):
    key = jax.random.fold_in(key, 23)
    first_key = jax.random.fold_in(key, 0)
    values = 2.5 * jax.random.normal(first_key, (LAT, QH * RD), jnp.float32)
    return jnp.clip(values, -15.0, 15.0).astype(jnp.bfloat16)


def set_ends(array, key, low, largest):
    extent = array.shape
    place = [jax.random.randint(jax.random.fold_in(key, axis), (), 0, extent[axis]) for axis in range(len(extent))]
    array = array.at[tuple(place)].set(low)
    longest = extent.index(max(extent))
    place[longest] = (place[longest] + 1) % extent[longest]
    return array.at[tuple(place)].set(largest)


def steps_of(own_key, shape, cuts, low, top_value):
    gain = 1.0
    for axis_at, shards_of in cuts:
        draws = jax.random.uniform(jax.random.fold_in(jax.random.fold_in(own_key, 6), axis_at), (shards_of,), jnp.float32, low / len(cuts), top_value / len(cuts))
        gain = gain * jnp.repeat(jnp.exp(draws), shape[axis_at] // shards_of).reshape((-1,) + (1,) * (len(shape) - 1 - axis_at))
    return gain


def length_profile(count, total, most, lean):
    weights = [(1 << 20) // math.isqrt(rank ** lean) + 1 for rank in range(2, count + 1)]
    surplus, holding = total - most - (count - 1), [1] * (count - 1)
    while surplus > 0:
        movable = [i for i in range(count - 1) if holding[i] < most]
        whole, remaining = sum([weights[i] for i in movable]), surplus
        for i in movable:
            extra = min(most - holding[i], max(1, remaining * weights[i] // whole), surplus)
            holding[i] = holding[i] + extra
            surplus = surplus - extra
    return np.array([most] + holding)


def ragged(own_key, count, total, limit, skew):
    if count == 2:
        one = jax.random.randint(own_key, (), max(1, total - limit), min(limit, total - 1) + 1)
        return jnp.stack([one, total - one])
    sizes = jnp.asarray(length_profile(count, total, limit, skew), jnp.int32)
    pairs = (count - 1) // 2
    giver, sink = sizes[1:1 + 2 * pairs:2], sizes[2:2 + 2 * pairs:2]
    slack = jnp.minimum(giver - 1, limit - sink)
    passed = jax.random.randint(jax.random.fold_in(own_key, 1), (pairs,), 0, 1 << 20) % (slack + 1)
    sizes = sizes.at[1:1 + 2 * pairs:2].set(giver - passed).at[2:2 + 2 * pairs:2].set(sink + passed)
    return sizes[jax.random.permutation(jax.random.fold_in(own_key, 2), count)]


def gaussian(own_key, dims, width, most, pieces=(), held_as=jnp.bfloat16):
    result = jax.random.normal(own_key, dims, jnp.float32) * width
    if len(pieces) > 0:
        result = steps_of(own_key, dims, pieces, -0.22, 0.18) * result
    return jnp.clip(result, min=-most, max=most).astype(held_as)


def setup_inputs(seed: int = 0, part: int = 0) -> dict:
    keys = jax.random.split(jax.random.key(seed), 12)
    own_keys = jax.random.split(jax.random.fold_in(keys[11], part), 12)
    patches = gaussian(own_keys[0], (TILES, PATCHES, D), 1.0, 6.0, ((0, 32),))
    counts = ragged(own_keys[1], IMAGES, TILES, MAX_TILES, 2).astype(jnp.int32)
    owner_pick = set_ends(jax.random.randint(own_keys[2], (IMAGES,), 0, 60), jax.random.fold_in(own_keys[2], 1), 0, 59).astype(jnp.int32)
    ln_gain = jnp.clip(1.0 + 0.18 * jax.random.normal(keys[3], (D,), jnp.float32), 0.1, 1.9)
    ln_bias = gaussian(keys[4], (D,), 0.5, 3.0, (), jnp.float32)
    w_qkv = gaussian(keys[5], (D, 3 * HA * HS), D ** -0.5, 0.1875)
    w_out = gaussian(keys[6], (HA * HS, D), (HA * HS) ** -0.5, 0.25)
    ctx_gain = jnp.clip(1.0 + 0.18 * jax.random.normal(keys[7], (D,), jnp.float32), 0.1, 1.9)
    w_kv = gaussian(keys[8], (D, 2 * KVH * RD), D ** -0.5, 0.1875)
    latent_queries = draw_latent_queries(jax.random.fold_in(keys[11], 71), part)
    latent_kv = draw_latent_kv(jax.random.fold_in(keys[11], 71), part)
    return dict(patches=patches, counts=counts, owner_pick=owner_pick, ln_gain=ln_gain, ln_bias=ln_bias, w_qkv=w_qkv, w_out=w_out, ctx_gain=ctx_gain, w_kv=w_kv, latent_queries=latent_queries, latent_kv=latent_kv)


NORM_EPS = 1e-06
EMPTY_PEAK = -1e+30

def as_wide(rounded):
    return lax.optimization_barrier(rounded).astype(jnp.float32)

def layer_norm(row_values, norm_gain, norm_bias):
    average = lax.optimization_barrier(jnp.mean(row_values, axis=-1, keepdims=True))
    centred = row_values - average
    variance = lax.optimization_barrier(jnp.mean(centred * centred, axis=-1, keepdims=True))
    return centred * lax.rsqrt(variance + NORM_EPS) * norm_gain + norm_bias

def tower_layer(tiles, ln_gain, ln_bias, w_qkv, w_out):
    tile_count, tile_rows, model_width = tiles.shape
    inner_width = w_out.shape[0]
    head_count = inner_width // HS
    widened = tiles.astype(jnp.float32)
    normed = layer_norm(widened, ln_gain, ln_bias).astype(jnp.bfloat16)
    packed = jnp.einsum('npd,de->npe', as_wide(normed), w_qkv.astype(jnp.float32), precision=lax.Precision.HIGHEST).astype(jnp.bfloat16)
    packed = as_wide(packed).reshape(tile_count, tile_rows, 3, head_count, HS)
    scores = jnp.einsum('nqhe,nkhe->nhqk', packed[:, :, 0], packed[:, :, 1], precision=lax.Precision.HIGHEST) * HS ** (-0.5)
    attention = jax.nn.softmax(scores, axis=-1).astype(jnp.bfloat16)
    mixture = jnp.einsum('nhqk,nkhe->nqhe', as_wide(attention), packed[:, :, 2], precision=lax.Precision.HIGHEST).astype(jnp.bfloat16)
    mixture = as_wide(mixture).reshape(tile_count, tile_rows, inner_width)
    update = jnp.einsum('npe,ed->npd', mixture, w_out.astype(jnp.float32), precision=lax.Precision.HIGHEST)
    return (widened + update).astype(jnp.bfloat16)

def context_values(features, ctx_gain, w_kv):
    widened = features.astype(jnp.float32)
    scaled = widened * lax.rsqrt(lax.optimization_barrier(jnp.mean(widened * widened, axis=-1, keepdims=True)) + NORM_EPS) * ctx_gain
    scaled = scaled.astype(jnp.bfloat16)
    return jnp.einsum('npd,de->npe', as_wide(scaled), w_kv.astype(jnp.float32), precision=lax.Precision.HIGHEST).astype(jnp.bfloat16)

def block_states(latent_queries, blocks):
    block_count, key_count = (blocks.shape[0], blocks.shape[1])
    key_width = KVH * RD
    group_size = QH // KVH
    widened = as_wide(blocks)
    key_vectors = widened[:, :, :key_width].reshape(block_count, key_count, KVH, RD)
    value_vectors = widened[:, :, key_width:].reshape(block_count, key_count, KVH, RD)
    grouped = latent_queries.astype(jnp.float32).reshape(LAT, KVH, group_size, RD)
    scores = jnp.einsum('lkgd,tpkd->tlkgp', grouped, key_vectors, precision=lax.Precision.HIGHEST) * RD ** (-0.5)
    top_score = lax.optimization_barrier(jnp.max(scores, axis=-1))
    weights = jnp.exp(scores - top_score[..., None])
    weight_sum = lax.optimization_barrier(jnp.sum(weights, axis=-1))
    rounded = as_wide(weights.astype(jnp.bfloat16))
    weighted = jnp.einsum('tlkgp,tpkd->tlkgd', rounded, value_vectors, precision=lax.Precision.HIGHEST)
    return (top_score.reshape(block_count, LAT, QH), weight_sum.reshape(block_count, LAT, QH), weighted.reshape(block_count, LAT, QH, RD))

def image_of(tile_ids, image_ends):
    return lax.optimization_barrier(jnp.sum((image_ends[None, :] <= tile_ids[..., None]).astype(jnp.int32), axis=-1))

def reference(patches, counts, owner_pick, ln_gain, ln_bias, w_qkv, w_out, ctx_gain, w_kv, latent_queries, latent_kv):
    features = tower_layer(patches, ln_gain, ln_bias, w_qkv, w_out)
    context = context_values(features, ctx_gain, w_kv)
    tile_top, tile_sum, tile_acc = block_states(latent_queries, context)
    lat_top, lat_sum, lat_acc = block_states(latent_queries, latent_kv[None])
    image_ends = jnp.cumsum(counts).astype(jnp.int32)
    image_starts = (image_ends - counts).astype(jnp.int32)
    tile_ids = jnp.arange(TILES, dtype=jnp.int32)
    tile_image = image_of(tile_ids, image_ends)

    def one_image(image_index):
        member = (tile_image == image_index)[:, None, None]
        overall = jnp.maximum(lax.optimization_barrier(jnp.max(jnp.where(member, tile_top, EMPTY_PEAK), axis=0)), lat_top[0])
        scale_tiles = jnp.where(member, jnp.exp(tile_top - overall[None]), 0.0)
        scale_lat = jnp.exp(lat_top[0] - overall)
        total = lax.optimization_barrier(jnp.sum(scale_tiles * tile_sum, axis=0)) + scale_lat * lat_sum[0]
        acc = lax.optimization_barrier(jnp.sum(scale_tiles[..., None] * tile_acc, axis=0)) + scale_lat[..., None] * lat_acc[0]
        return (acc / total[..., None]).reshape(LAT, QH * RD)
    image_ids = jnp.arange(IMAGES, dtype=jnp.int32)
    results = lax.map(one_image, image_ids)
    first_dev = image_starts // TILE_DEV
    last_dev = (image_ends - 1) // TILE_DEV
    owner_dev = first_dev + owner_pick % (last_dev - first_dev + 1)
    rank = jnp.where(image_of(owner_dev * TILE_DEV, image_ends) == image_ids, 0, 1).astype(jnp.int32)
    slots = (owner_dev * 2 + rank).astype(jnp.int32)
    placed = jnp.zeros((2 * N_BAL, LAT, QH * RD), jnp.float32).at[slots].set(results)
    return placed.reshape(N_BAL, 2, LAT, QH * RD).astype(jnp.bfloat16)
```

```python
import functools
import math

import jax
import jax.numpy as jnp
from jax import lax
from jax.experimental import pallas as pl
from jax.experimental.pallas import tpu as pltpu
from jax.sharding import PartitionSpec as P

D = 1152
HA = 8
HS = 72
PATCHES = 256
QH = 16
KVH = 4
RD = 96
LAT = 64
T = 2
IMAGES = 16
REACH = 4
ROWS = T * PATCHES
KW = KVH * RD
EPS = 1e-6
NEG = -1e30
LOG2E = math.log2(math.e)
C_TOWER = LOG2E / math.sqrt(HS)
C_RES = LOG2E / math.sqrt(RD)
MESH = pl.DeviceIdType.MESH
F32 = jnp.float32
BF = jnp.bfloat16
NT = (((1,), (1,)), ((), ()))
KWIN = ((0, 128), (0, 256), (128, 256), (256, 128))


def lanes(shape):
    return lax.broadcasted_iota(jnp.int32, shape, len(shape) - 1)


def dot(a, b):
    return jnp.dot(a, b, preferred_element_type=F32)


def dot_nt(a, b):
    return lax.dot_general(a, b, NT, preferred_element_type=F32)


def roll(x, shift):
    shift = shift % x.shape[-1]
    return x if shift == 0 else pltpu.roll(x, shift, 1)


def kernel(
    patches,
    counts,
    picks,
    ln_gain,
    ln_bias,
    w_qkv,
    w_out,
    ctx_gain,
    w_kv,
    latent_q,
    latent_kv,
    out,
    xb,
    wq,
    wo,
    wk,
    nb,
    pk,
    qr,
    mix,
    fg,
    cx,
    vk,
    qx,
    lq,
    lkv,
    send_o,
    send_s,
    got_o,
    got_s,
    lat_o,
    lat_s,
    load_sem,
    send_sem,
    recv_sem,
):
    me = lax.axis_index("bal")
    dp = lax.axis_index("dp")
    n = lax.axis_size("bal")
    right = lax.rem(me + 1, n)
    left = lax.rem(me + n - 1, n)
    sides = ((dp, right), (dp, left))

    loads = []

    def load(src, dst):
        copy = pltpu.make_async_copy(src, dst, load_sem.at[len(loads)])
        copy.start()
        loads.append(copy)
        return copy

    x_loads = [load(patches.at[t], xb.at[pl.ds(t * PATCHES, PATCHES)]) for t in range(T)]
    cuts = [(j * 256, min(256, 3 * HA * HS - j * 256)) for j in range(7)]
    q_loads = [load(w_qkv.at[pl.ds(a, w)], wq.at[pl.ds(a, w)]) for a, w in cuts]
    lq_load = load(latent_q, lq)
    lkv_load = load(latent_kv, lkv)
    wo_load = load(w_out, wo)
    wk_load = load(w_kv, wk)

    barrier = pltpu.get_barrier_semaphore()
    for side in sides:
        pl.semaphore_signal(barrier, inc=1, device_id=side, device_id_type=MESH)

    gain = ln_gain[...].reshape(1, D)
    bias = ln_bias[...].reshape(1, D)

    RB = 16
    for t in range(T):
        x_loads[t].wait()

        def norm(i, _, t=t):
            rows = pl.ds(pl.multiple_of(t * PATCHES + i * RB, RB), RB)
            x = xb[rows, :].astype(F32)
            mean = jnp.mean(x, axis=-1, keepdims=True)
            c = x - mean
            var = jnp.mean(c * c, axis=-1, keepdims=True)
            nb[rows, :] = (c * lax.rsqrt(var + EPS) * gain + bias).astype(BF)
            return 0

        lax.fori_loop(0, PATCHES // RB, norm, 0, unroll=2)

    for j, (a, w) in enumerate(cuts):
        q_loads[j].wait()
        res = dot_nt(nb[...], wq[pl.ds(a, w), :]).astype(BF)
        if w < 256:
            res = jnp.concatenate([res, jnp.zeros((ROWS, 256 - w), BF)], axis=1)
        pk[:, pl.ds(a, 256)] = res

    def shift_q(i, _):
        rows = pl.ds(pl.multiple_of(i * 32, 32), 32)
        ln = lanes((32, 128))
        before = jnp.zeros((32, 128), F32)
        for j in range(5):
            now = roll(pk[rows, pl.ds(j * 128, 128)].astype(F32), 64)
            qr[rows, pl.ds(j * 128, 128)] = jnp.where(ln < 64, before, now).astype(BF)
            before = now
        return 0

    lax.fori_loop(0, ROWS // 32, shift_q, 0)

    def tower(t, _):
        rows = pl.ds(pl.multiple_of(t * PATCHES, PATCHES), PATCHES)
        ln = lanes((PATCHES, 256))
        before = jnp.zeros((PATCHES, 128), F32)
        for i in range(HA // 2):
            q = qr[rows, pl.ds(128 * i, 256)]
            k = pk[rows, pl.ds(512 + 128 * i, 256)]
            v = pk[rows, pl.ds(1152 + 128 * i, 256)]
            mixed = jnp.zeros((PATCHES, 256), F32)
            for h in range(2):
                lo = 64 + 16 * i + HS * h
                mine = jnp.logical_and(ln >= lo, ln < lo + HS)
                s = dot_nt(jnp.where(mine, q, jnp.zeros_like(q)), k)
                top = jnp.max(s, axis=-1, keepdims=True)
                e = jnp.exp2((s - top) * C_TOWER)
                total = jnp.sum(e, axis=-1, keepdims=True)
                o = dot(e.astype(BF), v) * (1.0 / total)
                lo = 16 * i + HS * h
                mixed = jnp.where(jnp.logical_and(ln >= lo, ln < lo + HS), o, mixed)
            mix[rows, pl.ds(128 * i, 128)] = (before + mixed[:, :128]).astype(BF)
            before = mixed[:, 128:]
        mix[rows, pl.ds(512, 128)] = before.astype(BF)
        return 0

    lax.fori_loop(0, T, tower, 0)

    wo_load.wait()
    gain_c = ctx_gain[...].reshape(1, D)
    square = jnp.zeros((ROWS, 128), F32)
    for a in range(0, D, 256):
        w = min(256, D - a)
        f = dot(mix[:, : HA * HS], wo[:, pl.ds(a, w)]) + xb[:, pl.ds(a, w)].astype(F32)
        f = f.astype(BF).astype(F32)
        for b in range(0, w, 128):
            square = square + f[:, b : b + 128] * f[:, b : b + 128]
        fg[:, pl.ds(a, w)] = (f * gain_c[:, a : a + w]).astype(BF)
    factor = lax.rsqrt(jnp.sum(square, axis=-1, keepdims=True) * (1.0 / D) + EPS)

    wk_load.wait()
    for a in range(0, 2 * KW, 256):
        cx[:, pl.ds(a, 256)] = (dot(fg[...], wk[:, pl.ds(a, 256)]) * factor).astype(BF)

    lq_load.wait()
    lkv_load.wait()
    ln = lanes((LAT, 128))
    for k in range(KVH):
        qt = [lq[:, pl.ds(k * KW + 128 * j, 128)].astype(F32) for j in range(3)]
        first, width = KWIN[k]
        for g in range(4):
            parts = []
            for b in range(first, first + width, 128):
                move = b - RD * k + RD * g
                acc = jnp.zeros((LAT, 128), F32)
                for j in range(3):
                    lo = max(RD * k, b, 128 * j - move + b) - b
                    hi = min(RD * k + RD, b + 128, 128 * j + 128 - move + b) - b
                    if hi > lo:
                        moved = roll(qt[j], 128 * j - move)
                        acc = jnp.where(jnp.logical_and(ln >= lo, ln < hi), moved, acc)
                parts.append(acc)
            qx[k, pl.ds(g * LAT, LAT), pl.ds(0, width)] = jnp.concatenate(parts, axis=1).astype(BF)

    def head_values(ref, rows, count, k):
        ln = lanes((count, 128))
        lo = RD * k
        a = lo // 128
        shift = -(lo - 128 * a)
        one = roll(ref[rows, pl.ds(KW + 128 * a, 128)].astype(F32), shift)
        if lo + RD > 128 * (a + 1):
            two = roll(ref[rows, pl.ds(KW + 128 * (a + 1), 128)].astype(F32), shift)
            one = jnp.where(ln < 128 + shift, one, two)
        return one.astype(BF)

    def head_state(ref, rows, count, k):
        first, width = KWIN[k]
        s = dot_nt(qx[k, :, pl.ds(0, width)], ref[rows, pl.ds(first, width)])
        top = jnp.max(s, axis=-1, keepdims=True)
        e = jnp.exp2((s - top) * C_RES)
        total = jnp.sum(e, axis=-1, keepdims=True)
        o = dot(e.astype(BF), head_values(ref, rows, count, k)) * (1.0 / total)
        return top * C_RES + jnp.log2(total), o

    def dense(o):
        p = [roll(o[LAT * g : LAT * g + LAT], RD * g) for g in range(4)]
        return jnp.concatenate(
            [
                jnp.where(ln < 96, p[0], p[1]),
                jnp.where(ln < 64, p[1], p[2]),
                jnp.where(ln < 32, p[2], p[3]),
            ],
            axis=1,
        )

    def compact(table, lse, k):
        for g in range(4):
            column = jnp.broadcast_to(lse[LAT * g : LAT * g + LAT], (LAT, 128))
            table = jnp.where(ln == 4 * k + g, column, table)
        return table

    ends = []
    run = jnp.int32(0)
    for i in range(IMAGES):
        run = run + counts[i]
        ends.append(run)

    def image_of(tile):
        found = jnp.int32(0)
        for i in range(IMAGES):
            found = found + jnp.where(ends[i] <= tile, 1, 0)
        return found

    firsts = {d: image_of(2 * (me + d)) for d in range(0, REACH + 1)}
    lasts = {d: jnp.where(me + d < 0, -1, image_of(2 * (me + d) + 1)) for d in range(-REACH, 1)}
    img0, img1 = firsts[0], lasts[0]
    same = img0 == img1

    def owner_of(image):
        begin, end, pick = jnp.int32(0), jnp.int32(0), jnp.int32(0)
        for i in range(IMAGES):
            hit = image == i
            begin = jnp.where(hit, ends[i] - counts[i], begin)
            end = jnp.where(hit, ends[i], end)
            pick = jnp.where(hit, picks[i], pick)
        first, last = begin // 2, (end - 1) // 2
        return first + lax.rem(pick, last - first + 1)

    def flag(cond):
        return jnp.where(cond, F32(1.0), F32(0.0))

    def block(cond):
        return jnp.where(cond, F32(0.0), F32(NEG))

    has0 = flag(owner_of(img0) == me)
    has1 = flag(jnp.logical_and(owner_of(img1) == me, jnp.logical_not(same)))
    both = block(same)

    def copies(side, r, c):
        if c < KVH:
            src = send_o.at[side, c] if r == 0 else got_o.at[side, r - 1, c]
            dst = got_o.at[side, r, c]
        else:
            src = send_s.at[side] if r == 0 else got_s.at[side, r - 1]
            dst = got_s.at[side, r]
        return pltpu.make_async_remote_copy(
            src_ref=src,
            dst_ref=dst,
            send_sem=send_sem.at[side, r, c],
            recv_sem=recv_sem.at[side, r, c],
            device_id=sides[side],
            device_id_type=MESH,
        )

    tables = [jnp.zeros((LAT, 128), F32) for _ in range(3)]
    pl.semaphore_wait(barrier, 2)
    for k in range(KVH):
        l0, o0 = head_state(cx, pl.ds(0, PATCHES), PATCHES, k)
        l1, o1 = head_state(cx, pl.ds(PATCHES, PATCHES), PATCHES, k)
        pairs = ((l1, l0 + both), (l1 + both, l0))
        for side, (a, b) in enumerate(pairs):
            top = jnp.maximum(a, b)
            ea, eb = jnp.exp2(a - top), jnp.exp2(b - top)
            total = ea + eb
            inv = 1.0 / total
            tables[side] = compact(tables[side], top + jnp.log2(total), k)
            send_o[side, k] = dense(o1 * (ea * inv) + o0 * (eb * inv)).astype(BF)
            copies(side, 0, k).start()
        ll, ol = head_state(lkv, pl.ds(0, LAT), LAT, k)
        tables[2] = compact(tables[2], ll, k)
        lat_o[k] = dense(ol)
    for side in range(2):
        send_s[side] = tables[side]
        copies(side, 0, KVH).start()
    lat_s[...] = tables[2]

    order = (KVH,) + tuple(range(KVH))
    for r in range(REACH):
        for c in order:
            for side in range(2):
                copies(side, r, c).wait_recv()
                if r + 1 < REACH:
                    copies(side, r + 1, c).start()

    lr = [got_s[0, r] + block(lasts[-1 - r] == img0) for r in range(REACH)]
    ll0 = [got_s[1, r] + block(firsts[1 + r] == img0) for r in range(REACH)]
    ll1 = [got_s[1, r] + block(firsts[1 + r] == img1) for r in range(REACH)]
    slots = (
        [tables[1], tables[2]] + lr + ll0,
        [tables[0], tables[2]] + ll1,
    )
    weights = []
    for slot, has in zip(slots, (has0, has1)):
        top = functools.reduce(jnp.maximum, slot)
        es = [jnp.exp2(v - top) for v in slot]
        inv = has / functools.reduce(jnp.add, es)
        weights.append([e * inv for e in es])

    def spread(w, k):
        p = [jnp.broadcast_to(w[:, 4 * k + g : 4 * k + g + 1], (LAT, 128)) for g in range(4)]
        return jnp.concatenate(
            [jnp.where(ln < 96, p[0], p[1]), jnp.where(ln < 64, p[1], p[2]), jnp.where(ln < 32, p[2], p[3])],
            axis=1,
        )

    for k in range(KVH):
        sources = (
            [send_o[1, k], lat_o[k]]
            + [got_o[0, r, k] for r in range(REACH)]
            + [got_o[1, r, k] for r in range(REACH)],
            [send_o[0, k], lat_o[k]] + [got_o[1, r, k] for r in range(REACH)],
        )
        for slot in range(2):
            total = jnp.zeros((LAT, KW), F32)
            for w, o in zip(weights[slot], sources[slot]):
                total = total + spread(w, k) * o.astype(F32)
            out[0, slot, :, pl.ds(k * KW, KW)] = total.astype(BF)

    for r in range(REACH):
        for c in order:
            for side in range(2):
                copies(side, r, c).wait_send()


def per_device(*args):
    args = list(args)
    args[5] = args[5].T
    hbm = pl.BlockSpec(memory_space=pl.ANY)
    vmem = pl.BlockSpec(memory_space=pltpu.VMEM)
    smem = pl.BlockSpec(memory_space=pltpu.SMEM)
    return pl.pallas_call(
        kernel,
        out_shape=jax.ShapeDtypeStruct((1, 2, LAT, QH * RD), BF),
        in_specs=[hbm, smem, smem, vmem, vmem, hbm, hbm, vmem, hbm, hbm, hbm],
        out_specs=vmem,
        scratch_shapes=[
            pltpu.VMEM((ROWS, D), BF),
            pltpu.VMEM((3 * HA * HS, D), BF),
            pltpu.VMEM((HA * HS, D), BF),
            pltpu.VMEM((D, 2 * KW), BF),
            pltpu.VMEM((ROWS, D), BF),
            pltpu.VMEM((ROWS, 1792), BF),
            pltpu.VMEM((ROWS, 640), BF),
            pltpu.VMEM((ROWS, 640), BF),
            pltpu.VMEM((ROWS, D), BF),
            pltpu.VMEM((ROWS, 2 * KW), BF),
            pltpu.VMEM((16, 128), BF),
            pltpu.VMEM((KVH, 4 * LAT, 256), BF),
            pltpu.VMEM((LAT, QH * RD), BF),
            pltpu.VMEM((LAT, 2 * KW), BF),
            pltpu.VMEM((2, KVH, LAT, KW), BF),
            pltpu.VMEM((2, LAT, 128), F32),
            pltpu.VMEM((2, REACH, KVH, LAT, KW), BF),
            pltpu.VMEM((2, REACH, LAT, 128), F32),
            pltpu.VMEM((KVH, LAT, KW), F32),
            pltpu.VMEM((LAT, 128), F32),
            pltpu.SemaphoreType.DMA((16,)),
            pltpu.SemaphoreType.DMA((2, REACH, KVH + 1)),
            pltpu.SemaphoreType.DMA((2, REACH, KVH + 1)),
        ],
        compiler_params=pltpu.CompilerParams(
            collective_id=0, has_side_effects=True, vmem_limit_bytes=60 * 2**20
        ),
        cost_estimate=pl.CostEstimate(flops=4_300_000_000, bytes_accessed=9_000_000, transcendentals=1_600_000),
        name="tower_resampler",
    )(*args)


def solution(mesh):
    return jax.shard_map(
        per_device,
        mesh=mesh,
        in_specs=(
            P(("dp", "bal"), None, None),
            P("dp"),
            P("dp"),
            P(),
            P(),
            P(),
            P(),
            P(),
            P(),
            P(),
            P(),
        ),
        out_specs=P(("dp", "bal"), None, None, None),
        check_vma=False,
    )
```

```python
import functools
import math

import jax
import jax.numpy as jnp
from jax import lax
from jax.experimental import pallas as pl
from jax.experimental.pallas import tpu as pltpu
from jax.sharding import PartitionSpec as P

D = 1152
HA = 8
HS = 72
PATCHES = 256
QH = 16
KVH = 4
RD = 96
LAT = 64
T = 2
IMAGES = 16
REACH = 4
ROWS = T * PATCHES
KW = KVH * RD
WA = HA * HS
EPS = 1e-6
NEG = -1e30
LOG2E = math.log2(math.e)
C_TOWER = LOG2E / math.sqrt(HS)
C_RES = LOG2E / math.sqrt(RD)
MESH = pl.DeviceIdType.MESH
F32 = jnp.float32
BF = jnp.bfloat16
NT = (((1,), (1,)), ((), ()))
KWIN = ((0, 128), (0, 256), (128, 256), (256, 128))
STAT = 96


def lanes(shape):
    return lax.broadcasted_iota(jnp.int32, shape, len(shape) - 1)


def dot(a, b):
    return jnp.dot(a, b, preferred_element_type=F32)


def dot_nt(a, b):
    return lax.dot_general(a, b, NT, preferred_element_type=F32)


def roll(x, shift):
    shift = shift % x.shape[-1]
    return x if shift == 0 else pltpu.roll(x, shift, 1)


def kernel(
    patches,
    counts_hbm,
    picks_hbm,
    ln_gain_hbm,
    ln_bias_hbm,
    w_qkv,
    w_out,
    ctx_gain_hbm,
    w_kv,
    latent_q,
    latent_kv,
    out,
    counts,
    picks,
    ln_gain,
    ln_bias,
    ctx_gain,
    xb,
    wq,
    wo,
    wk,
    nb,
    qv,
    kt,
    mix,
    fg,
    cx,
    qx,
    lq,
    lkv,
    send_o,
    send_s,
    got_o,
    got_s,
    lat_o,
    acc_r,
    acc_l,
    acc_1,
    ob,
    load_sem,
    send_sem,
    recv_sem,
    stat_send_sem,
    stat_recv_sem,
    out_sem,
    group_sem,
    factor,
    tops,
    sums,
    wt,
    last_r,
    last_l,
):
    me = lax.axis_index("bal")
    dp = lax.axis_index("dp")
    n = lax.axis_size("bal")

    loads = []

    def load(src, dst):
        copy = pltpu.make_async_copy(src, dst, load_sem.at[len(loads)])
        copy.start()
        loads.append(copy)
        return copy

    def wait(c):
        c.wait()

    x_loads = [load(patches.at[0], xb.at[pl.ds(0, PATCHES)])]
    small = [load(ln_gain_hbm, ln_gain), load(ln_bias_hbm, ln_bias)]
    x_loads.append(load(patches.at[1], xb.at[pl.ds(PATCHES, PATCHES)]))

    def group(g):
        row = pl.multiple_of(256 * g + jnp.where(g >= 2, 704, 0), 64)
        rows = pl.ds(row, 256)
        return pltpu.make_async_copy(w_qkv.at[rows], wq.at[rows], group_sem.at[g])

    for g in range(2):
        group(g).start()
    end_loads = [load(w_qkv.at[pl.ds(a, 64)], wq.at[pl.ds(a, 64)]) for a in (512, 2 * WA)]
    for g in range(2, 4):
        group(g).start()
    k_load = load(w_qkv.at[pl.ds(WA, WA)], wq.at[pl.ds(WA, WA)])
    wo_load = load(w_out, wo.at[pl.ds(64, WA)])
    small += [load(ctx_gain_hbm, ctx_gain), load(counts_hbm, counts), load(picks_hbm, picks)]
    lq_load = load(latent_q, lq)
    lkv_load = load(latent_kv, lkv)
    wk_load = load(w_kv, wk)

    got_o[...] = jnp.zeros_like(got_o)
    got_s[...] = jnp.zeros_like(got_s)
    tops[...] = jnp.zeros_like(tops)
    sums[...] = jnp.zeros_like(sums)
    wo[pl.ds(0, 64), :] = jnp.zeros((64, D), BF)
    kt[pl.ds(WA, 64), :] = jnp.zeros((64, ROWS), BF)

    def exists(side, distance):
        return me + distance < n if side == 0 else me - distance >= 0

    def at(side, distance):
        return (dp, me + distance if side == 0 else me - distance)

    barrier = pltpu.get_barrier_semaphore()
    for side in range(2):
        for distance in range(1, REACH + 1):

            @pl.when(exists(side, distance))
            def _(side=side, distance=distance):
                pl.semaphore_signal(barrier, inc=1, device_id=at(side, distance), device_id_type=MESH)

    def greeted():
        pl.semaphore_wait(barrier, jnp.minimum(me, REACH) + jnp.minimum(n - 1 - me, REACH))

    wait(small[0])
    wait(small[1])
    gain = ln_gain[...].reshape(1, D)
    bias = ln_bias[...].reshape(1, D)
    for c in x_loads:
        wait(c)

    def norm(i, _):
        rows = pl.ds(pl.multiple_of(i * 32, 32), 32)
        x = xb[rows, :].astype(F32)
        mean = jnp.mean(x, axis=-1, keepdims=True)
        c = x - mean
        var = jnp.mean(c * c, axis=-1, keepdims=True)
        nb[rows, :] = (c * lax.rsqrt(var + EPS) * gain + bias).astype(BF)
        return 0

    lax.fori_loop(0, ROWS // 32, norm, 0, unroll=4)

    def project(g, _):
        group(g).wait()
        rows = pl.ds(pl.multiple_of(256 * g + jnp.where(g >= 2, 704, 0), 64), 256)
        columns = pl.ds(pl.multiple_of(256 * g + jnp.where(g >= 2, 128, 0), 128), 256)
        qv[:, columns] = dot_nt(nb[...], wq[rows, :]).astype(BF)
        return 0

    lax.fori_loop(0, 4, project, 0)
    for c in end_loads:
        wait(c)
    ends_w = jnp.concatenate([wq[pl.ds(512, 64), :], wq[pl.ds(2 * WA, 64), :]], axis=0)
    qv[:, pl.ds(512, 128)] = dot_nt(nb[...], ends_w).astype(BF)
    wait(k_load)

    def project_keys(t, _):
        rows = pl.ds(pl.multiple_of(t * PATCHES, PATCHES), PATCHES)
        kt[pl.ds(0, WA), rows] = dot_nt(wq[pl.ds(WA, WA), :], nb[rows, :]).astype(BF)
        return 0

    lax.fori_loop(0, T, project_keys, 0)

    def tower(t, _):
        rows = pl.ds(pl.multiple_of(t * PATCHES, PATCHES), PATCHES)
        ln = lanes((PATCHES, 256))
        before = jnp.zeros((PATCHES, 128), F32)
        for i in range(HA // 2):
            q = qv[rows, pl.ds(128 * i, 256)]
            k = kt[pl.ds(128 * i, 256), rows]
            v = qv[rows, pl.ds(512 + 128 * i, 256)]
            mixed = jnp.zeros((PATCHES, 256), F32)
            for h in range(2):
                lo = 16 * i + HS * h
                mine = jnp.logical_and(ln >= lo, ln < lo + HS)
                s = dot(jnp.where(mine, q, jnp.zeros_like(q)), k)
                top = jnp.max(s, axis=-1, keepdims=True)
                e = jnp.exp2((s - top) * C_TOWER)
                total = jnp.sum(e, axis=-1, keepdims=True)
                o = dot(e.astype(BF), v) * (1.0 / total)
                lo += 64
                mixed = jnp.where(jnp.logical_and(ln >= lo, ln < lo + HS), o, mixed)
            mix[rows, pl.ds(128 * i, 128)] = (before + mixed[:, :128]).astype(BF)
            before = mixed[:, 128:]
        mix[rows, pl.ds(512, 128)] = before.astype(BF)
        return 0

    lax.fori_loop(0, T, tower, 0)

    wait(wo_load)
    wait(small[2])
    gain_c = ctx_gain[...].reshape(1, D)
    square = jnp.zeros((ROWS, 128), F32)
    for a in range(0, D, 256):
        w = min(256, D - a)
        f = dot(mix[...], wo[:, pl.ds(a, w)]) + xb[:, pl.ds(a, w)].astype(F32)
        f = f.astype(BF).astype(F32)
        for b in range(0, w, 128):
            square = square + f[:, b : b + 128] * f[:, b : b + 128]
        fg[:, pl.ds(a, w)] = (f * gain_c[:, a : a + w]).astype(BF)
    factor[...] = jnp.broadcast_to(
        lax.rsqrt(jnp.sum(square, axis=-1, keepdims=True) * (1.0 / D) + EPS), (ROWS, 128)
    )

    wait(wk_load)

    for a in range(0, 2 * KW, 256):
        c = dot(fg[...], wk[:, pl.ds(a, 256)])
        for b in (0, 128):
            cx[:, pl.ds(a + b, 128)] = (c[:, b : b + 128] * factor[...]).astype(BF)

    wait(lq_load)
    wait(lkv_load)
    ln = lanes((LAT, 128))
    for k in range(KVH):
        qt = [lq[:, pl.ds(k * KW + 128 * j, 128)].astype(F32) for j in range(3)]
        first, width = KWIN[k]
        for g in range(4):
            parts = []
            for b in range(first, first + width, 128):
                move = b - RD * k + RD * g
                acc = jnp.zeros((LAT, 128), F32)
                for j in range(3):
                    lo = max(RD * k - b, 0, 128 * j - move)
                    hi = min(RD * k + RD - b, 128, 128 * j + 128 - move)
                    if hi > lo:
                        moved = roll(qt[j], 128 * j - move)
                        acc = jnp.where(jnp.logical_and(ln >= lo, ln < hi), moved, acc)
                parts.append(acc)
            qx[k, pl.ds(g * LAT, LAT), pl.ds(0, width)] = jnp.concatenate(parts, axis=1).astype(BF)

    wait(small[3])
    wait(small[4])
    ends = []
    run = jnp.int32(0)
    for i in range(IMAGES):
        run = run + counts[i]
        ends.append(run)

    def image_of(tile):
        found = jnp.int32(0)
        for i in range(IMAGES):
            found = found + jnp.where(ends[i] <= tile, 1, 0)
        return found

    def flag(cond):
        return jnp.where(cond, F32(1.0), F32(0.0))

    def block(cond):
        return jnp.where(cond, F32(0.0), F32(NEG))

    firsts = [image_of(2 * (me + d)) for d in range(0, REACH + 1)]
    lasts = [jnp.where(me - d < 0, -1, image_of(2 * (me - d) + 1)) for d in range(0, REACH + 1)]
    img0, img1 = firsts[0], lasts[0]
    same = img0 == img1
    samef = flag(same)

    def owner_of(image):
        begin, end, pick = jnp.int32(0), jnp.int32(0), jnp.int32(0)
        for i in range(IMAGES):
            hit = image == i
            begin = jnp.where(hit, ends[i] - counts[i], begin)
            end = jnp.where(hit, ends[i], end)
            pick = jnp.where(hit, picks[i], pick)
        first, last = begin // 2, (end - 1) // 2
        return first + lax.rem(pick, last - first + 1)

    has0 = flag(owner_of(img0) == me)
    has1 = flag(jnp.logical_and(owner_of(img1) == me, jnp.logical_not(same)))

    def values(ref, rows, count, k):
        ln = lanes((count, 128))
        a, shift = RD * k // 128, -(RD * k % 128)
        one = roll(ref[rows, pl.ds(KW + 128 * a, 128)].astype(F32), shift)
        if RD * k + RD > 128 * (a + 1):
            two = roll(ref[rows, pl.ds(KW + 128 * (a + 1), 128)].astype(F32), shift)
            one = jnp.where(ln < 128 + shift, one, two)
        return jnp.where(ln < RD, one, 1.0).astype(BF)

    def scores(ref, rows, k):
        first, width = KWIN[k]
        s = dot_nt(qx[k, :, pl.ds(0, width)], ref[rows, pl.ds(first, width)])
        return s, jnp.max(s, axis=-1, keepdims=True)

    def weigh(ref, rows, count, k, s, top):
        e = jnp.exp2((s - top) * C_RES)
        return dot(e.astype(BF), values(ref, rows, count, k))

    def merge(parts):
        return jnp.concatenate(
            [
                jnp.where(ln < 96, parts[0], parts[1]),
                jnp.where(ln < 64, parts[1], parts[2]),
                jnp.where(ln < 32, parts[2], parts[3]),
            ],
            axis=1,
        )

    def dense(o):
        return merge([roll(o[LAT * g : LAT * g + LAT], RD * g) for g in range(4)])

    def compact(table, o, k):
        new = table[...]
        for g in range(4):
            part = jnp.broadcast_to(o[LAT * g : LAT * g + LAT], (LAT, 128))
            new = jnp.where(ln == STAT + 4 * k + g, part, new)
        table[...] = new

    def data(side, r, c):
        return pltpu.make_async_remote_copy(
            src_ref=send_o.at[side, c] if r == 0 else got_o.at[side, r - 1, c],
            dst_ref=got_o.at[side, r, c],
            send_sem=send_sem.at[side, r, c],
            recv_sem=recv_sem.at[side, r, c],
            device_id=at(side, 1),
            device_id_type=MESH,
        )

    def sends(side, r):
        return jnp.logical_and(exists(side, 1), exists(1 - side, r))

    def receives(side, r):
        return exists(1 - side, r + 1)

    def stats(side, r):
        slot = side * REACH + r
        return pltpu.make_async_remote_copy(
            src_ref=send_s.at[side],
            dst_ref=got_s.at[pl.ds(16 * slot, 16)],
            send_sem=stat_send_sem.at[side, r],
            recv_sem=stat_recv_sem.at[side, r],
            device_id=at(side, r + 1),
            device_id_type=MESH,
        )

    greeted()
    t0, t1 = pl.ds(0, PATCHES), pl.ds(PATCHES, PATCHES)

    def head(k):

        s0, top0 = scores(cx, t0, k)
        s1, top1 = scores(cx, t1, k)
        both = jnp.maximum(top0, top1)
        top0 = jnp.where(same, both, top0)
        top1 = jnp.where(same, both, top1)
        a0 = weigh(cx, t0, PATCHES, k, s0, top0)
        a1 = weigh(cx, t1, PATCHES, k, s1, top1)
        for side, (top, a) in enumerate(((top1, a1 + samef * a0), (top0, a0 + samef * a1))):
            send_o[side, k] = dense(a).astype(BF)

            @pl.when(sends(side, 0))
            def _(side=side):
                data(side, 0, k).start()

            compact(tops.at[side], top, k)
            compact(sums.at[side], a, k)

        sl, topl = scores(lkv, pl.ds(0, LAT), k)
        al = weigh(lkv, pl.ds(0, LAT), LAT, k, sl, topl)
        compact(tops.at[2], topl, k)
        compact(sums.at[2], al, k)
        lat_o[k] = dense(al)

    for k in range(KVH):
        head(k)

    for side in range(2):
        both = jnp.concatenate([tops[side] * C_RES, sums[side]], axis=0)
        send_s[side] = both.T[STAT : STAT + QH]
        for r in range(REACH):

            @pl.when(exists(side, r + 1))
            def _(side=side, r=r):
                stats(side, r).start()

    def arrive(side, r, c):
        @pl.when(receives(side, r))
        def _():
            data(side, r, c).wait_recv()

        if r + 1 < REACH:

            @pl.when(sends(side, r + 1))
            def _():
                data(side, r + 1, c).start()

    def forward(r):
        for side in range(2):

            def step(c, _, side=side):
                arrive(side, r, c)
                return 0

            lax.fori_loop(0, KVH, step, 0)

    forward(0)
    forward(1)

    for side in range(2):
        for r in range(REACH):

            @pl.when(exists(1 - side, r + 1))
            def _(side=side, r=r):
                stats(side, r).wait_recv()

    table = got_s[...].T
    all_tops, all_sums = table[:LAT], table[LAT:]

    def of_source(x, slot):
        return roll(x, STAT - 16 * slot)

    own = [(tops[side] * C_RES, sums[side]) for side in range(2)]
    latent = (tops[2] * C_RES, sums[2])
    r_src = [
        (of_source(all_tops, r) + block(lasts[r + 1] == img0), of_source(all_sums, r)) for r in range(REACH)
    ]
    l_src = [
        (of_source(all_tops, REACH + r) + block(firsts[r + 1] == img1), of_source(all_sums, REACH + r))
        for r in range(REACH)
    ]
    apart = block(jnp.logical_not(same))
    together = block(same)
    slots = (
        [own[1], latent] + r_src + [(t + together, s) for t, s in l_src],
        [own[0], latent] + [(t + apart, s) for t, s in l_src],
    )
    weights = []
    for slot in slots:
        top = functools.reduce(jnp.maximum, [t for t, _ in slot])
        es = [jnp.exp2(t - top) for t, _ in slot]
        inv = 1.0 / functools.reduce(jnp.add, [e * s for e, (_, s) in zip(es, slot)])
        weights.append([e * inv for e in es])
    w_own0, w_lat0 = weights[0][:2]
    w_own1, w_lat1 = weights[1][:2]
    w_r = weights[0][2 : 2 + REACH]
    w_l = [a + b for a, b in zip(weights[0][2 + REACH :], weights[1][2:])]

    for i, w in enumerate([w_own0, w_lat0, w_own1, w_lat1] + w_r + w_l):
        wt[i] = w

    def spread(i, k):
        w = pltpu.roll(wt[i], lax.rem(128 - 4 * k, 128), 1)
        return merge([jnp.broadcast_to(w[:, STAT + g : STAT + g + 1], (LAT, 128)) for g in range(4)])

    def start(k, _):
        lat = lat_o[k]
        acc_r[k] = spread(0, k) * send_o[1, k].astype(F32) + spread(1, k) * lat
        acc_1[k] = spread(2, k) * send_o[0, k].astype(F32) + spread(3, k) * lat
        acc_l[k] = jnp.zeros((LAT, KW), F32)
        return 0

    lax.fori_loop(0, KVH, start, 0)

    def absorb(r):
        def step(k, _):
            acc_r[k] += spread(4 + r, k) * got_o[0, r, k].astype(F32)
            acc_l[k] += spread(8 + r, k) * got_o[1, r, k].astype(F32)
            return 0

        lax.fori_loop(0, KVH, step, 0)

    forward(2)
    for r in range(REACH - 1):
        absorb(r)

    def last_weights(k, _):
        last_r[k] = spread(4 + REACH - 1, k)
        last_l[k] = spread(8 + REACH - 1, k)
        return 0

    lax.fori_loop(0, KVH, last_weights, 0)

    def result(k):
        return pltpu.make_async_copy(ob.at[k], out.at[0, :, :, pl.ds(pl.multiple_of(k * KW, 128), KW)], out_sem.at[k])

    def finish_r(k, _):
        arrive(0, REACH - 1, k)
        acc_r[k] += last_r[k] * got_o[0, REACH - 1, k].astype(F32)
        return 0

    def finish_l(k, _):
        arrive(1, REACH - 1, k)
        from_l = acc_l[k] + last_l[k] * got_o[1, REACH - 1, k].astype(F32)
        ob[k, 0] = ((acc_r[k] + samef * from_l) * has0).astype(BF)
        ob[k, 1] = ((acc_1[k] + (1.0 - samef) * from_l) * has1).astype(BF)
        result(k).start()
        return 0

    lax.fori_loop(0, KVH, finish_r, 0)
    lax.fori_loop(0, KVH, finish_l, 0)

    for side in range(2):
        for r in range(REACH):

            @pl.when(exists(side, r + 1))
            def _(side=side, r=r):
                stats(side, r).wait_send()

            for c in range(KVH):

                @pl.when(sends(side, r))
                def _(side=side, r=r, c=c):
                    data(side, r, c).wait_send()

    for k in range(KVH):
        result(k).wait()


def per_device(*args):
    args = list(args)
    args[5] = args[5].T
    hbm = pl.BlockSpec(memory_space=pl.ANY)
    vmem, smem, dma = pltpu.VMEM, pltpu.SMEM, pltpu.SemaphoreType.DMA
    return pl.pallas_call(
        kernel,
        out_shape=jax.ShapeDtypeStruct((1, 2, LAT, QH * RD), BF),
        in_specs=[hbm] * 11,
        out_specs=hbm,
        scratch_shapes=[
            smem((IMAGES,), jnp.int32),
            smem((IMAGES,), jnp.int32),
            vmem((D,), F32),
            vmem((D,), F32),
            vmem((D,), F32),
            vmem((ROWS, D), BF),
            vmem((3 * WA, D), BF),
            vmem((640, D), BF),
            vmem((D, 2 * KW), BF),
            vmem((ROWS, D), BF),
            vmem((ROWS, D), BF),
            vmem((640, ROWS), BF),
            vmem((ROWS, 640), BF),
            vmem((ROWS, D), BF),
            vmem((ROWS, 2 * KW), BF),
            vmem((KVH, 4 * LAT, 256), BF),
            vmem((LAT, QH * RD), BF),
            vmem((LAT, 2 * KW), BF),
            vmem((2, KVH, LAT, KW), BF),
            vmem((2, QH, 128), F32),
            vmem((2, REACH, KVH, LAT, KW), BF),
            vmem((2 * REACH * 16, 128), F32),
            vmem((KVH, LAT, KW), F32),
            vmem((KVH, LAT, KW), F32),
            vmem((KVH, LAT, KW), F32),
            vmem((KVH, LAT, KW), F32),
            vmem((KVH, 2, LAT, KW), BF),
            dma((24,)),
            dma((2, REACH, KVH)),
            dma((2, REACH, KVH)),
            dma((2, REACH)),
            dma((2, REACH)),
            dma((KVH,)),
            dma((4,)),
            vmem((ROWS, 128), F32),
            vmem((3, LAT, 128), F32),
            vmem((3, LAT, 128), F32),
            vmem((12, LAT, 128), F32),
            vmem((KVH, LAT, KW), F32),
            vmem((KVH, LAT, KW), F32),
        ],
        compiler_params=pltpu.CompilerParams(
            collective_id=0, has_side_effects=True, vmem_limit_bytes=60 * 2**20
        ),
        cost_estimate=pl.CostEstimate(flops=4_300_000_000, bytes_accessed=9_000_000, transcendentals=1_600_000),
        name="tower_resampler",
    )(*args)


def solution(mesh):
    return jax.shard_map(
        per_device,
        mesh=mesh,
        in_specs=(
            P(("dp", "bal"), None, None),
            P("dp"),
            P("dp"),
            P(),
            P(),
            P(),
            P(),
            P(),
            P(),
            P(),
            P(),
        ),
        out_specs=P(("dp", "bal"), None, None, None),
        check_vma=False,
    )
```

```python
import functools
import math

import jax
import jax.numpy as jnp
from jax import lax
from jax.experimental import pallas as pl
from jax.experimental.pallas import tpu as pltpu
from jax.sharding import PartitionSpec as P

D = 1152
HA = 8
HS = 72
PATCHES = 256
QH = 16
KVH = 4
RD = 96
LAT = 64
T = 2
IMAGES = 16
REACH = 4
ROWS = T * PATCHES
KW = KVH * RD
WA = HA * HS
EPS = 1e-6
NEG = -1e30
LOG2E = math.log2(math.e)
C_TOWER = LOG2E / math.sqrt(HS)
C_RES = LOG2E / math.sqrt(RD)
MESH = pl.DeviceIdType.MESH
F32 = jnp.float32
BF = jnp.bfloat16
NT = (((1,), (1,)), ((), ()))
KWIN = ((0, 128), (0, 256), (128, 256), (256, 128))
STAT = 96


def lanes(shape):
    return lax.broadcasted_iota(jnp.int32, shape, len(shape) - 1)


def dot(a, b):
    return jnp.dot(a, b, preferred_element_type=F32)


def dot_nt(a, b):
    return lax.dot_general(a, b, NT, preferred_element_type=F32)


def roll(x, shift):
    shift = shift % x.shape[-1]
    return x if shift == 0 else pltpu.roll(x, shift, 1)


def kernel(
    patches,
    counts_hbm,
    picks_hbm,
    ln_gain_hbm,
    ln_bias_hbm,
    w_qkv,
    w_out,
    ctx_gain_hbm,
    w_kv,
    latent_q,
    latent_kv,
    out,
    counts,
    picks,
    ln_gain,
    ln_bias,
    ctx_gain,
    xb,
    wq,
    wo,
    wk,
    nb,
    qv,
    kt,
    mix,
    fg,
    cx,
    qx,
    lq,
    lkv,
    send_o,
    send_s,
    got_o,
    got_s,
    lat_o,
    acc_r,
    acc_l,
    acc_1,
    ob,
    load_sem,
    send_sem,
    recv_sem,
    stat_send_sem,
    stat_recv_sem,
    out_sem,
    group_sem,
    factor,
    tops,
    sums,
    wt,
    last_r,
    last_l,
):
    me = lax.axis_index("bal")
    dp = lax.axis_index("dp")
    n = lax.axis_size("bal")

    loads = []

    def load(src, dst):
        copy = pltpu.make_async_copy(src, dst, load_sem.at[len(loads)])
        copy.start()
        loads.append(copy)
        return copy

    def wait(c):
        c.wait()

    x_loads = [load(patches.at[0], xb.at[pl.ds(0, PATCHES)])]
    small = [load(ln_gain_hbm, ln_gain), load(ln_bias_hbm, ln_bias)]
    x_loads.append(load(patches.at[1], xb.at[pl.ds(PATCHES, PATCHES)]))

    def group(g):
        row = pl.multiple_of(256 * g + jnp.where(g >= 2, 704, 0), 64)
        rows = pl.ds(row, 256)
        return pltpu.make_async_copy(w_qkv.at[rows], wq.at[rows], group_sem.at[g])

    for g in range(2):
        group(g).start()
    end_loads = [load(w_qkv.at[pl.ds(a, 64)], wq.at[pl.ds(a, 64)]) for a in (512, 2 * WA)]
    for g in range(2, 4):
        group(g).start()
    k_load = load(w_qkv.at[pl.ds(WA, WA)], wq.at[pl.ds(WA, WA)])
    wo_load = load(w_out, wo.at[pl.ds(64, WA)])
    small += [load(ctx_gain_hbm, ctx_gain), load(counts_hbm, counts), load(picks_hbm, picks)]
    lq_load = load(latent_q, lq)
    lkv_load = load(latent_kv, lkv)
    wk_load = load(w_kv, wk)

    got_o[...] = jnp.zeros_like(got_o)
    got_s[...] = jnp.zeros_like(got_s)
    tops[...] = jnp.zeros_like(tops)
    sums[...] = jnp.zeros_like(sums)
    wo[pl.ds(0, 64), :] = jnp.zeros((64, D), BF)
    kt[pl.ds(WA, 64), :] = jnp.zeros((64, ROWS), BF)

    def exists(side, distance):
        return me + distance < n if side == 0 else me - distance >= 0

    def at(side, distance):
        return (dp, me + distance if side == 0 else me - distance)

    barrier = pltpu.get_barrier_semaphore()
    for side in range(2):
        for distance in range(1, REACH + 1):

            @pl.when(exists(side, distance))
            def _(side=side, distance=distance):
                pl.semaphore_signal(barrier, inc=1, device_id=at(side, distance), device_id_type=MESH)

    def greeted():
        pl.semaphore_wait(barrier, jnp.minimum(me, REACH) + jnp.minimum(n - 1 - me, REACH))

    wait(small[0])
    wait(small[1])
    gain = ln_gain[...].reshape(1, D)
    bias = ln_bias[...].reshape(1, D)
    for c in x_loads:
        wait(c)

    def norm(i, _):
        rows = pl.ds(pl.multiple_of(i * 32, 32), 32)
        x = xb[rows, :].astype(F32)
        mean = jnp.mean(x, axis=-1, keepdims=True)
        c = x - mean
        var = jnp.mean(c * c, axis=-1, keepdims=True)
        nb[rows, :] = (c * lax.rsqrt(var + EPS) * gain + bias).astype(BF)
        return 0

    lax.fori_loop(0, ROWS // 32, norm, 0, unroll=4)

    for g in range(4):
        group(g).wait()
    for c in end_loads:
        wait(c)
    wait(k_load)

    def project(t, _):
        rows = pl.ds(pl.multiple_of(t * PATCHES, PATCHES), PATCHES)
        x = nb[rows, :]
        for g in range(4):
            a, c = 256 * g + (704 if g >= 2 else 0), 256 * g + (128 if g >= 2 else 0)
            qv[rows, pl.ds(c, 256)] = dot_nt(x, wq[pl.ds(a, 256), :]).astype(BF)
        ends_w = jnp.concatenate([wq[pl.ds(512, 64), :], wq[pl.ds(2 * WA, 64), :]], axis=0)
        qv[rows, pl.ds(512, 128)] = dot_nt(x, ends_w).astype(BF)
        kt[pl.ds(0, WA), rows] = dot_nt(wq[pl.ds(WA, WA), :], x).astype(BF)
        return 0

    lax.fori_loop(0, T, project, 0)

    def tower(t, _):
        rows = pl.ds(pl.multiple_of(t * PATCHES, PATCHES), PATCHES)
        ln = lanes((PATCHES, 256))
        before = jnp.zeros((PATCHES, 128), F32)
        for i in range(HA // 2):
            q = qv[rows, pl.ds(128 * i, 256)]
            k = kt[pl.ds(128 * i, 256), rows]
            v = qv[rows, pl.ds(512 + 128 * i, 256)]
            mixed = jnp.zeros((PATCHES, 256), F32)
            for h in range(2):
                lo = 16 * i + HS * h
                mine = jnp.logical_and(ln >= lo, ln < lo + HS)
                s = dot(jnp.where(mine, q, jnp.zeros_like(q)), k)
                top = jnp.max(s, axis=-1, keepdims=True)
                e = jnp.exp2((s - top) * C_TOWER)
                total = jnp.sum(e, axis=-1, keepdims=True)
                o = dot(e.astype(BF), v) * (1.0 / total)
                lo += 64
                mixed = jnp.where(jnp.logical_and(ln >= lo, ln < lo + HS), o, mixed)
            mix[rows, pl.ds(128 * i, 128)] = (before + mixed[:, :128]).astype(BF)
            before = mixed[:, 128:]
        mix[rows, pl.ds(512, 128)] = before.astype(BF)
        return 0

    lax.fori_loop(0, T, tower, 0)

    wait(wo_load)
    wait(small[2])
    gain_c = ctx_gain[...].reshape(1, D)
    square = jnp.zeros((ROWS, 128), F32)
    for a in range(0, D, 256):
        w = min(256, D - a)
        f = dot(mix[...], wo[:, pl.ds(a, w)]) + xb[:, pl.ds(a, w)].astype(F32)
        f = f.astype(BF).astype(F32)
        for b in range(0, w, 128):
            square = square + f[:, b : b + 128] * f[:, b : b + 128]
        fg[:, pl.ds(a, w)] = (f * gain_c[:, a : a + w]).astype(BF)
    factor[...] = jnp.broadcast_to(
        lax.rsqrt(jnp.sum(square, axis=-1, keepdims=True) * (1.0 / D) + EPS), (ROWS, 128)
    )

    wait(wk_load)


    def context(t, _):
        rows = pl.ds(pl.multiple_of(t * PATCHES, PATCHES), PATCHES)
        for a in range(0, 2 * KW, 256):
            c = dot(fg[rows, :], wk[:, pl.ds(a, 256)])
            for b in (0, 128):
                cx[rows, pl.ds(a + b, 128)] = (c[:, b : b + 128] * factor[rows, :]).astype(BF)
        return 0

    lax.fori_loop(0, T, context, 0)

    wait(lq_load)
    wait(lkv_load)
    ln = lanes((LAT, 128))
    for k in range(KVH):
        qt = [lq[:, pl.ds(k * KW + 128 * j, 128)].astype(F32) for j in range(3)]
        first, width = KWIN[k]
        for g in range(4):
            parts = []
            for b in range(first, first + width, 128):
                move = b - RD * k + RD * g
                acc = jnp.zeros((LAT, 128), F32)
                for j in range(3):
                    lo = max(RD * k - b, 0, 128 * j - move)
                    hi = min(RD * k + RD - b, 128, 128 * j + 128 - move)
                    if hi > lo:
                        moved = roll(qt[j], 128 * j - move)
                        acc = jnp.where(jnp.logical_and(ln >= lo, ln < hi), moved, acc)
                parts.append(acc)
            qx[k, pl.ds(g * LAT, LAT), pl.ds(0, width)] = jnp.concatenate(parts, axis=1).astype(BF)

    wait(small[3])
    wait(small[4])
    ends = []
    run = jnp.int32(0)
    for i in range(IMAGES):
        run = run + counts[i]
        ends.append(run)

    def image_of(tile):
        found = jnp.int32(0)
        for i in range(IMAGES):
            found = found + jnp.where(ends[i] <= tile, 1, 0)
        return found

    def flag(cond):
        return jnp.where(cond, F32(1.0), F32(0.0))

    def block(cond):
        return jnp.where(cond, F32(0.0), F32(NEG))

    firsts = [image_of(2 * (me + d)) for d in range(0, REACH + 1)]
    lasts = [jnp.where(me - d < 0, -1, image_of(2 * (me - d) + 1)) for d in range(0, REACH + 1)]
    img0, img1 = firsts[0], lasts[0]
    same = img0 == img1
    samef = flag(same)

    def owner_of(image):
        begin, end, pick = jnp.int32(0), jnp.int32(0), jnp.int32(0)
        for i in range(IMAGES):
            hit = image == i
            begin = jnp.where(hit, ends[i] - counts[i], begin)
            end = jnp.where(hit, ends[i], end)
            pick = jnp.where(hit, picks[i], pick)
        first, last = begin // 2, (end - 1) // 2
        return first + lax.rem(pick, last - first + 1)

    has0 = flag(owner_of(img0) == me)
    has1 = flag(jnp.logical_and(owner_of(img1) == me, jnp.logical_not(same)))

    def values(ref, rows, count, k):
        ln = lanes((count, 128))
        a, shift = RD * k // 128, -(RD * k % 128)
        one = roll(ref[rows, pl.ds(KW + 128 * a, 128)].astype(F32), shift)
        if RD * k + RD > 128 * (a + 1):
            two = roll(ref[rows, pl.ds(KW + 128 * (a + 1), 128)].astype(F32), shift)
            one = jnp.where(ln < 128 + shift, one, two)
        return jnp.where(ln < RD, one, 1.0).astype(BF)

    def scores(ref, rows, k):
        first, width = KWIN[k]
        s = dot_nt(qx[k, :, pl.ds(0, width)], ref[rows, pl.ds(first, width)])
        return s, jnp.max(s, axis=-1, keepdims=True)

    def weigh(ref, rows, count, k, s, top):
        e = jnp.exp2((s - top) * C_RES)
        return dot(e.astype(BF), values(ref, rows, count, k))

    def merge(parts):
        return jnp.concatenate(
            [
                jnp.where(ln < 96, parts[0], parts[1]),
                jnp.where(ln < 64, parts[1], parts[2]),
                jnp.where(ln < 32, parts[2], parts[3]),
            ],
            axis=1,
        )

    def dense(o):
        return merge([roll(o[LAT * g : LAT * g + LAT], RD * g) for g in range(4)])

    def compact(table, o, k):
        new = table[...]
        for g in range(4):
            part = jnp.broadcast_to(o[LAT * g : LAT * g + LAT], (LAT, 128))
            new = jnp.where(ln == STAT + 4 * k + g, part, new)
        table[...] = new

    def data(side, r, c):
        return pltpu.make_async_remote_copy(
            src_ref=send_o.at[side, c] if r == 0 else got_o.at[side, r - 1, c],
            dst_ref=got_o.at[side, r, c],
            send_sem=send_sem.at[side, r, c],
            recv_sem=recv_sem.at[side, r, c],
            device_id=at(side, 1),
            device_id_type=MESH,
        )

    def sends(side, r):
        return jnp.logical_and(exists(side, 1), exists(1 - side, r))

    def receives(side, r):
        return exists(1 - side, r + 1)

    def stats(side, r):
        slot = side * REACH + r
        return pltpu.make_async_remote_copy(
            src_ref=send_s.at[side],
            dst_ref=got_s.at[pl.ds(16 * slot, 16)],
            send_sem=stat_send_sem.at[side, r],
            recv_sem=stat_recv_sem.at[side, r],
            device_id=at(side, r + 1),
            device_id_type=MESH,
        )

    greeted()
    t0, t1 = pl.ds(0, PATCHES), pl.ds(PATCHES, PATCHES)

    def head(k):

        s0, top0 = scores(cx, t0, k)
        s1, top1 = scores(cx, t1, k)
        both = jnp.maximum(top0, top1)
        top0 = jnp.where(same, both, top0)
        top1 = jnp.where(same, both, top1)
        a0 = weigh(cx, t0, PATCHES, k, s0, top0)
        a1 = weigh(cx, t1, PATCHES, k, s1, top1)
        for side, (top, a) in enumerate(((top1, a1 + samef * a0), (top0, a0 + samef * a1))):
            send_o[side, k] = dense(a).astype(BF)

            @pl.when(sends(side, 0))
            def _(side=side):
                data(side, 0, k).start()

            compact(tops.at[side], top, k)
            compact(sums.at[side], a, k)

    for k in range(KVH):
        head(k)

    for side in range(2):
        both = jnp.concatenate([tops[side] * C_RES, sums[side]], axis=0)
        send_s[side] = both.T[STAT : STAT + QH]
        for r in range(REACH):

            @pl.when(exists(side, r + 1))
            def _(side=side, r=r):
                stats(side, r).start()

    def arrive(side, r, c):
        @pl.when(receives(side, r))
        def _():
            data(side, r, c).wait_recv()

        if r + 1 < REACH:

            @pl.when(sends(side, r + 1))
            def _():
                data(side, r + 1, c).start()

    def forward(r):
        def step(c, _):
            for side in range(2):
                arrive(side, r, c)
            return 0

        lax.fori_loop(0, KVH, step, 0)

    forward(0)

    def latent_head(k):
        sl, topl = scores(lkv, pl.ds(0, LAT), k)
        al = weigh(lkv, pl.ds(0, LAT), LAT, k, sl, topl)
        compact(tops.at[2], topl, k)
        compact(sums.at[2], al, k)
        lat_o[k] = dense(al)

    for k in range(KVH):
        latent_head(k)

    forward(1)

    for side in range(2):
        for r in range(REACH):

            @pl.when(exists(1 - side, r + 1))
            def _(side=side, r=r):
                stats(side, r).wait_recv()

    table = got_s[...].T
    all_tops, all_sums = table[:LAT], table[LAT:]

    def of_source(x, slot):
        return roll(x, STAT - 16 * slot)

    own = [(tops[side] * C_RES, sums[side]) for side in range(2)]
    latent = (tops[2] * C_RES, sums[2])
    r_src = [
        (of_source(all_tops, r) + block(lasts[r + 1] == img0), of_source(all_sums, r)) for r in range(REACH)
    ]
    l_src = [
        (of_source(all_tops, REACH + r) + block(firsts[r + 1] == img1), of_source(all_sums, REACH + r))
        for r in range(REACH)
    ]
    apart = block(jnp.logical_not(same))
    together = block(same)
    slots = (
        [own[1], latent] + r_src + [(t + together, s) for t, s in l_src],
        [own[0], latent] + [(t + apart, s) for t, s in l_src],
    )
    weights = []
    for slot in slots:
        top = functools.reduce(jnp.maximum, [t for t, _ in slot])
        es = [jnp.exp2(t - top) for t, _ in slot]
        inv = 1.0 / functools.reduce(jnp.add, [e * s for e, (_, s) in zip(es, slot)])
        weights.append([e * inv for e in es])
    w_own0, w_lat0 = weights[0][:2]
    w_own1, w_lat1 = weights[1][:2]
    w_r = weights[0][2 : 2 + REACH]
    w_l = [a + b for a, b in zip(weights[0][2 + REACH :], weights[1][2:])]

    for i, w in enumerate([w_own0, w_lat0, w_own1, w_lat1] + w_r + w_l):
        wt[i] = w

    def spread(i, k):
        w = pltpu.roll(wt[i], lax.rem(128 - 4 * k, 128), 1)
        return merge([jnp.broadcast_to(w[:, STAT + g : STAT + g + 1], (LAT, 128)) for g in range(4)])

    def start(k, _):
        lat = lat_o[k]
        acc_r[k] = spread(0, k) * send_o[1, k].astype(F32) + spread(1, k) * lat
        acc_1[k] = spread(2, k) * send_o[0, k].astype(F32) + spread(3, k) * lat
        acc_l[k] = jnp.zeros((LAT, KW), F32)
        return 0

    lax.fori_loop(0, KVH, start, 0)

    def absorb(r):
        def step(k, _):
            acc_r[k] += spread(4 + r, k) * got_o[0, r, k].astype(F32)
            acc_l[k] += spread(8 + r, k) * got_o[1, r, k].astype(F32)
            return 0

        lax.fori_loop(0, KVH, step, 0)

    forward(2)
    for r in range(REACH - 1):
        absorb(r)

    def last_weights(k, _):
        last_r[k] = spread(4 + REACH - 1, k)
        last_l[k] = spread(8 + REACH - 1, k)
        return 0

    lax.fori_loop(0, KVH, last_weights, 0)

    def result(k):
        return pltpu.make_async_copy(ob.at[k], out.at[0, :, :, pl.ds(pl.multiple_of(k * KW, 128), KW)], out_sem.at[k])

    def finish_r(k, _):
        arrive(0, REACH - 1, k)
        acc_r[k] += last_r[k] * got_o[0, REACH - 1, k].astype(F32)
        return 0

    def finish_l(k, _):
        arrive(1, REACH - 1, k)
        from_l = acc_l[k] + last_l[k] * got_o[1, REACH - 1, k].astype(F32)
        ob[k, 0] = ((acc_r[k] + samef * from_l) * has0).astype(BF)
        ob[k, 1] = ((acc_1[k] + (1.0 - samef) * from_l) * has1).astype(BF)
        result(k).start()
        return 0

    lax.fori_loop(0, KVH, finish_r, 0)
    lax.fori_loop(0, KVH, finish_l, 0)

    for side in range(2):
        for r in range(REACH):

            @pl.when(exists(side, r + 1))
            def _(side=side, r=r):
                stats(side, r).wait_send()

            for c in range(KVH):

                @pl.when(sends(side, r))
                def _(side=side, r=r, c=c):
                    data(side, r, c).wait_send()

    for k in range(KVH):
        result(k).wait()


def per_device(*args):
    args = list(args)
    args[5] = args[5].T
    hbm = pl.BlockSpec(memory_space=pl.ANY)
    vmem, smem, dma = pltpu.VMEM, pltpu.SMEM, pltpu.SemaphoreType.DMA
    return pl.pallas_call(
        kernel,
        out_shape=jax.ShapeDtypeStruct((1, 2, LAT, QH * RD), BF),
        in_specs=[hbm] * 11,
        out_specs=hbm,
        scratch_shapes=[
            smem((IMAGES,), jnp.int32),
            smem((IMAGES,), jnp.int32),
            vmem((D,), F32),
            vmem((D,), F32),
            vmem((D,), F32),
            vmem((ROWS, D), BF),
            vmem((3 * WA, D), BF),
            vmem((640, D), BF),
            vmem((D, 2 * KW), BF),
            vmem((ROWS, D), BF),
            vmem((ROWS, D), BF),
            vmem((640, ROWS), BF),
            vmem((ROWS, 640), BF),
            vmem((ROWS, D), BF),
            vmem((ROWS, 2 * KW), BF),
            vmem((KVH, 4 * LAT, 256), BF),
            vmem((LAT, QH * RD), BF),
            vmem((LAT, 2 * KW), BF),
            vmem((2, KVH, LAT, KW), BF),
            vmem((2, QH, 128), F32),
            vmem((2, REACH, KVH, LAT, KW), BF),
            vmem((2 * REACH * 16, 128), F32),
            vmem((KVH, LAT, KW), F32),
            vmem((KVH, LAT, KW), F32),
            vmem((KVH, LAT, KW), F32),
            vmem((KVH, LAT, KW), F32),
            vmem((KVH, 2, LAT, KW), BF),
            dma((24,)),
            dma((2, REACH, KVH)),
            dma((2, REACH, KVH)),
            dma((2, REACH)),
            dma((2, REACH)),
            dma((KVH,)),
            dma((4,)),
            vmem((ROWS, 128), F32),
            vmem((3, LAT, 128), F32),
            vmem((3, LAT, 128), F32),
            vmem((12, LAT, 128), F32),
            vmem((KVH, LAT, KW), F32),
            vmem((KVH, LAT, KW), F32),
        ],
        compiler_params=pltpu.CompilerParams(
            collective_id=0, has_side_effects=True, vmem_limit_bytes=60 * 2**20
        ),
        cost_estimate=pl.CostEstimate(flops=4_300_000_000, bytes_accessed=9_000_000, transcendentals=1_600_000),
        name="tower_resampler",
    )(*args)


def solution(mesh):
    return jax.shard_map(
        per_device,
        mesh=mesh,
        in_specs=(
            P(("dp", "bal"), None, None),
            P("dp"),
            P("dp"),
            P(),
            P(),
            P(),
            P(),
            P(),
            P(),
            P(),
            P(),
        ),
        out_specs=P(("dp", "bal"), None, None, None),
        check_vma=False,
    )
```
